512 devices in a mesh: dp: 64 (over x, z), mp: 8 (over y, core).
Axes of the slice: x: 4, y: 4, z: 16, core: 2. Of those that a mesh axis runs over, the one named last changes fastest.
Arguments:
- query: bfloat16 [32768, 2048], P('dp', 'mp'), may hold values from -2.5 to 2.5
- key: bfloat16 [32768, 2048], P('dp', 'mp'), may hold values from -2.5 to 2.5
- value: bfloat16 [32768, 2048], P('dp', 'mp'), may hold values from -6 to 6
- cotangent: bfloat16 [32768, 4096], P('dp', 'mp'), may hold values from -16 to 16
- weight_out: bfloat16 [4096, 2048], P('dp', 'mp'), may hold values from -0.125 to 0.125
- keep_attn: int32 [32, 64], P('mp', 'dp'), may hold values from 0 to 65279
- keep_out: int32 [64, 4096], P('dp', 'mp'), may hold values from 0 to 65279
- doc_lengths: int32 [64, 8], P('dp'), may hold values from 1 to 256, 512 in all within a row
Outputs:
- grad_query: bfloat16 [32768, 2048], P('dp', 'mp')
- grad_key: bfloat16 [32768, 2048], P('dp', 'mp')
- grad_value: bfloat16 [32768, 2048], P('dp', 'mp')
- grad_weight: float32 [4096, 2048], P('dp', 'mp')
The draws below stay inside these ranges and needn't reach their ends.
All inputs are finite; a program needn't handle non-finite values.
Results may differ from the reference program's by a relative error of at most 0.02.
Values may be sent and summed in bfloat16 or wider, within the bound.
A program may use at most 64 MiB of HBM per device.

```python
import math
import jax
import jax.numpy as jnp
import numpy as np
from jax import lax

D = 4096
HEADS = 32
DK = 64
SEQ = 512
DOCS = 8
INNER = 2048
ROWS = 64
TOKENS = 32768


def draw_query(key, part):
    own = jax.random.fold_in(key, 11)
    return (0.35 * jax.random.truncated_normal(own, -7.0, 7.0, (TOKENS, INNER), jnp.float32)).astype(jnp.bfloat16)


def draw_key(key, part):
    own = jax.random.fold_in(key, 23)
    return (0.35 * jax.random.truncated_normal(own, -7.0, 7.0, (TOKENS, INNER), jnp.float32)).astype(jnp.bfloat16)


def set_ends(result, stream_key, low, high):
    spot = [jax.random.randint(jax.random.fold_in(stream_key, axis), (), 0, length) for axis, length in enumerate(result.shape)]
    longest = result.shape.index(max(result.shape))
    next_to = spot[:longest] + [(spot[longest] + 1) % result.shape[longest]] + spot[longest + 1:]
    return result.at[tuple(spot)].set(low).at[tuple(next_to)].set(high)


def strengthened(drawn, key, source, target, shards_of, factor):
    def block_of(position):
        return (jnp.arange(drawn.shape[position]) // (drawn.shape[position] // shards_of)).reshape((-1,) + (1,) * (drawn.ndim - 1 - position))

    first = jax.random.permutation(key, shards_of)[block_of(target)]
    second = (block_of(target) + shards_of // 2) % shards_of
    return jnp.where((block_of(source) == first) | (block_of(source) == second), factor * drawn, drawn)


def steps_of(stream_key, dims, pieces, low, high):
    loudness, own = 1.0, jax.random.fold_in(stream_key, 6)
    for dim, parts in pieces:
        draws = jnp.exp(jax.random.uniform(jax.random.fold_in(own, dim), (parts,), jnp.float32, low / len(pieces), high / len(pieces)))
        loudness = loudness * jnp.repeat(draws, dims[dim] // parts).reshape([-1 if axis == dim else 1 for axis in range(len(dims))])
    return loudness


def split_up(number_of, total, limit, slope):
    portions = [(1 << 20) // math.isqrt(grade ** slope) + 1 for grade in range(2, number_of + 1)]
    rest, given = total - limit - (number_of - 1), [1] * (number_of - 1)
    while rest > 0:
        candidates = [i for i in range(number_of - 1) if given[i] < limit]
        mass, remaining = sum([portions[i] for i in candidates]), rest
        for i in candidates:
            extra = min(limit - given[i], max(1, remaining * portions[i] // mass), rest)
            given[i] = given[i] + extra
            rest = rest - extra
    return np.array([limit] + given)


def ragged(own_key, count, total, limit, slope):
    if count == 2:
        one = jax.random.randint(own_key, (), max(1, total - limit), min(limit, total - 1) + 1)
        return jnp.stack([one, total - one])
    sizes = jnp.asarray(split_up(count, total, limit, slope), jnp.int32)
    couples = (count - 1) // 2
    source_of, receiver = sizes[1:1 + 2 * couples:2], sizes[2:2 + 2 * couples:2]
    room = jnp.minimum(source_of - 1, limit - receiver)
    shifted = jax.random.randint(jax.random.fold_in(own_key, 1), (couples,), 0, 1 << 20) % (room + 1)
    sizes = sizes.at[1:1 + 2 * couples:2].set(source_of - shifted).at[2:2 + 2 * couples:2].set(receiver + shifted)
    return sizes[jax.random.permutation(jax.random.fold_in(own_key, 2), count)]


def normal_values(key, extent, spread, most, shards=(), held_as=jnp.bfloat16):
    array = jax.random.normal(key, extent, jnp.float32) * spread
    if len(shards) > 0:
        array = steps_of(key, extent, shards, -0.22, 0.18) * array
    return jnp.clip(array, min=-most, max=most).astype(held_as)


def gaussian_with(key, dims, scale, bound, shards, heavy, kind=jnp.bfloat16):
    values = scale * jax.random.normal(key, dims, jnp.float32)
    if shards:
        values = values * steps_of(key, dims, shards, -0.22, 0.18)
    return jnp.clip(strengthened(values, jax.random.fold_in(key, 3), *heavy), -bound, bound).astype(kind)


def setup_inputs(seed: int = 0) -> dict:
    streams_of = jax.random.split(jax.random.key(seed), 9)
    return {
        "query": draw_query(jax.random.fold_in(streams_of[8], 71), 0),
        "key": draw_key(jax.random.fold_in(streams_of[8], 71), 0),
        "value": normal_values(streams_of[2], (TOKENS, INNER), 1.0, 6.0, ((0, 64), (1, 8))),
        "cotangent": gaussian_with(streams_of[3], (TOKENS, D), 1.0, 16.0, ((0, 64), (1, 8)), (0, 1, 64, 4.0)),
        "weight_out": normal_values(streams_of[4], (D, INNER), INNER ** -0.5, 0.125, ((0, 64), (1, 8))),
        "keep_attn": set_ends(jax.random.randint(streams_of[5], (HEADS, ROWS), 0, 65280), jax.random.fold_in(streams_of[5], 1), 0, 65279).astype(jnp.int32),
        "keep_out": set_ends(jax.random.randint(streams_of[6], (ROWS, D), 0, 65280), jax.random.fold_in(streams_of[6], 1), 0, 65279).astype(jnp.int32),
        "doc_lengths": jax.vmap(lambda own: ragged(own, DOCS, SEQ, SEQ // 2, 2))(jax.random.split(streams_of[7], ROWS)).reshape((ROWS, DOCS)).astype(jnp.int32),
    }


DROP_SCALE = 1.0 / 0.9


def mix_bits(stream, first, second):
    x = stream * jnp.int32(-1640531535) + first * jnp.int32(668265263) + second * jnp.int32(374761393)
    x = x ^ lax.shift_right_logical(x, jnp.int32(16))
    x = x * jnp.int32(73244475)
    x = x ^ lax.shift_right_logical(x, jnp.int32(15))
    x = x * jnp.int32(-2048144789)
    x = x ^ lax.shift_right_logical(x, jnp.int32(16))
    return (((x & jnp.int32(65535)) % jnp.int32(10)) < jnp.int32(9)).astype(jnp.float32)


def segment_ids(lengths):
    ends = jnp.cumsum(lengths).astype(jnp.int32)
    places = jnp.arange(SEQ, dtype=jnp.int32)
    return jnp.sum((ends[None, :] <= places[:, None]).astype(jnp.int32), axis=1)


def row_pass(args):
    qrow, krow, vrow, grow, streams, lengths = args
    seg = segment_ids(lengths)
    same = seg[:, None] == seg[None, :]
    places = jnp.arange(SEQ, dtype=jnp.int32)
    keep = mix_bits(streams[:, None, None], places[None, :, None], places[None, None, :])
    qf = qrow.astype(jnp.float32)
    kf = krow.astype(jnp.float32)
    vf = vrow.astype(jnp.float32)
    gf = grow.astype(jnp.float32)
    scores = jnp.einsum("qhd,khd->hqk", qf, kf)
    scores = jnp.where(same[None], scores, -1e30)
    probs = jax.nn.softmax(scores, axis=-1)
    kept = (probs * keep * DROP_SCALE).astype(jnp.bfloat16)
    keptf = kept.astype(jnp.float32)
    context = jnp.einsum("hqk,khd->qhd", keptf, vf).astype(jnp.bfloat16)
    grad_value = jnp.einsum("hqk,qhd->khd", keptf, gf).astype(jnp.bfloat16)
    grad_probs = jnp.einsum("qhd,khd->hqk", gf, vf) * keep * DROP_SCALE
    delta = jnp.sum(probs * grad_probs, axis=-1, keepdims=True)
    grad_scores = (probs * (grad_probs - delta)).astype(jnp.bfloat16).astype(jnp.float32)
    grad_query = jnp.einsum("hqk,khd->qhd", grad_scores, kf).astype(jnp.bfloat16)
    grad_key = jnp.einsum("hqk,qhd->khd", grad_scores, qf).astype(jnp.bfloat16)
    return context, grad_query, grad_key, grad_value


def reference(query, key, value, cotangent, weight_out, keep_attn, keep_out, doc_lengths):
    places = jnp.arange(SEQ, dtype=jnp.int32)
    keep_o = mix_bits(keep_out[:, None, :], places[None, :, None], jnp.int32(0)).reshape(TOKENS, D)
    dropped = (cotangent.astype(jnp.float32) * keep_o * DROP_SCALE).astype(jnp.bfloat16)
    grad_context = jnp.dot(dropped, weight_out, preferred_element_type=jnp.float32).astype(jnp.bfloat16)

    def split_rows(x):
        return x.reshape(ROWS, SEQ, HEADS, DK)

    streams = jnp.transpose(keep_attn, (1, 0))
    context, grad_query, grad_key, grad_value = lax.map(
        row_pass, (split_rows(query), split_rows(key), split_rows(value), split_rows(grad_context), streams, doc_lengths))
    context = context.reshape(TOKENS, INNER)
    grad_weight = lax.dot_general(dropped, context, (((0,), (0,)), ((), ())), preferred_element_type=jnp.float32)
    return (grad_query.reshape(TOKENS, INNER), grad_key.reshape(TOKENS, INNER),
            grad_value.reshape(TOKENS, INNER), grad_weight)
```

```python
import jax
import jax.numpy as jnp
from jax import lax
from jax.experimental import pallas as pl
from jax.experimental.pallas import tpu as pltpu
from jax.sharding import PartitionSpec as P

MESH = pl.DeviceIdType.MESH
BF = jnp.bfloat16
F32 = jnp.float32
I32 = jnp.int32
DK = 64
SEQ = 512
HEADS = 4
FEAT = 256
NX, NY, NZ, NEAR = 4, 4, 16, 4
DROP = 0.9
DROP_SCALE = 1.0 / 0.9
TENTH = 429496730
TURN = -1717986918 + 1000
NINE = -(1 << 31) + 200000000


def kept_bits(x):
    x = x ^ lax.shift_right_logical(x, jnp.int32(16))
    x = x * jnp.int32(73244475)
    x = x ^ lax.shift_right_logical(x, jnp.int32(15))
    x = x * jnp.int32(-2048144789)
    x = x ^ lax.shift_right_logical(x, jnp.int32(16))
    return (x & jnp.int32(65535)) * jnp.int32(TENTH) + jnp.int32(TURN) >= jnp.int32(NINE)


def kernel(
    q_ref, k_ref, v_ref, cot_ref, w_ref, ka_ref, ko_ref, dl_ref,
    gq_ref, gk_ref, gv_ref, gw_ref,
    drt, wx, wt, qt_s, kt_s, vt_s, gt_s, g_s, ctxf, ctx, seg_s, spot_s, s_s, sp_s, kp_s, gs_s, gqt_s, gka, gva,
    hop_s, hop_r, fin_s, fin_r, own, near_s, near_r, far_s, far_r,
    ysend, yrecv, wxsend, wxrecv, wsend, wrecv, xsend, xrecv, nsend, nrecv, fsend, frecv,
):
    dp, mp = lax.axis_index("dp"), lax.axis_index("mp")
    x, z = dp // NZ, lax.rem(dp, NZ)
    y, c = mp // 2, lax.rem(mp, 2)
    near, far = lax.rem(z, NEAR), z // NEAR

    def at(dx=0, dy=0, dz=0, dc=0):
        px, py = lax.rem(x + dx + NX, NX), lax.rem(y + dy + NY, NY)
        pz, pc = lax.rem(z + dz + NZ, NZ), lax.rem(c + dc, 2)
        return (px * NZ + pz, py * 2 + pc)

    def near_peer(j):
        return (x * NZ + far * NEAR + lax.rem(near + j, NEAR), mp)

    core, yp, ym = at(dc=1), at(dy=1), at(dy=-1)
    xp, xm, x2, zp, zm = at(dx=1), at(dx=-1), at(dx=2), at(dz=1), at(dz=-1)
    near_peers = [near_peer(j) for j in range(1, NEAR)]
    far_peers = [at(dz=NEAR * j) for j in range(1, NEAR)]
    greeted = [core, yp, ym, xp, xm, x2, zp, zm] + near_peers + far_peers
    barrier = pltpu.get_barrier_semaphore()
    for peer in greeted:
        pl.semaphore_signal(barrier, inc=1, device_id=peer, device_id_type=MESH)

    pending = []

    def send(src, dst, ssem, rsem, peer):
        copy = pltpu.make_async_remote_copy(
            src_ref=src, dst_ref=dst, send_sem=ssem, recv_sem=rsem, device_id=peer, device_id_type=MESH
        )
        copy.start()
        pending.append(copy)

    def arrived(ref, ssem, rsem):
        pltpu.make_async_remote_copy(
            src_ref=ref, dst_ref=ref, send_sem=ssem, recv_sem=rsem, device_id=core, device_id_type=MESH
        ).wait_recv()

    spots = lax.broadcasted_iota(I32, (SEQ, 128), 0)
    first = spots * jnp.int32(668265263)
    for j in range(4):
        lanes = pl.ds(j * 128, 128)
        word = first + ko_ref[:, lanes] * jnp.int32(-1640531535)
        part = jnp.where(kept_bits(word), cot_ref[:, lanes].astype(F32) * DROP_SCALE, 0.0).astype(BF)
        drt[mp, j // 2, pl.ds((j % 2) * 128, 128), :] = part.T
    wx[x] = w_ref[...]

    pl.semaphore_wait(barrier, len(greeted))

    for i, peer in enumerate((xp, xm, x2)):
        send(wx.at[x], wx.at[x], wxsend.at[i], wxrecv.at[x], peer)
    ysends = [0]

    def ysend_to(block, piece, peer):
        ref = drt.at[block, piece]
        send(ref, ref, ysend.at[ysends[0]], yrecv.at[block, piece], peer)
        ysends[0] += 1

    for piece in range(2):
        for peer in (yp, ym, core):
            ysend_to(mp, piece, peer)

    def yblock(dy, dc=0):
        return lax.rem(y + dy + NY, NY) * 2 + lax.rem(c + dc, 2)

    def ywait(block, piece):
        arrived(drt.at[block, piece], ysend.at[0], yrecv.at[block, piece])

    def y_step(dy, piece):
        block = yblock(dy)
        ywait(block, piece)
        if dy == -1 and piece == 0:
            ysend_to(block, piece, yp)
        if dy == 1 and piece == 1:
            ysend_to(block, piece, ym)
        ysend_to(block, piece, core)

    wsends = [0]

    def ring_send(block, sub, peer):
        ref = wt.at[block, sub]
        send(ref, ref, wsend.at[wsends[0]], wrecv.at[block, sub], peer)
        wsends[0] += 1

    def ring_start():
        for j in (1, 2, 3):
            block = lax.rem(x + j, NX)
            arrived(wx.at[block], wxsend.at[0], wxrecv.at[block])
        own_w = jnp.concatenate([wx[j] for j in range(NX)], axis=0).T
        for sub in range(2):
            wt[z, sub] = own_w[sub * 128:(sub + 1) * 128]
            ring_send(z, sub, zp)
            ring_send(z, sub, zm)

    def ring_step(k):
        for sub in range(2):
            block = lax.rem(z - k + NZ, NZ)
            arrived(wt.at[block, sub], wsend.at[0], wrecv.at[block, sub])
            if k < NZ // 2:
                ring_send(block, sub, zp)
            if k < NZ // 2:
                block = lax.rem(z + k, NZ)
                arrived(wt.at[block, sub], wsend.at[0], wrecv.at[block, sub])
                if k < NZ // 2 - 1:
                    ring_send(block, sub, zm)

    ends, total = [], 0
    for j in range(8):
        total = total + dl_ref[0, j]
        ends.append(total)

    def segments(places):
        seg = jnp.zeros(places.shape, I32)
        for end in ends:
            seg = seg + (places >= end).astype(I32)
        return seg

    seg_s[...] = segments(spots)
    spot_s[...] = spots * jnp.int32(374761393)
    qt_s[...] = q_ref[...].T
    kt_s[...] = k_ref[...].T
    vt_s[...] = v_ref[...].T
    head_rows = lax.broadcasted_iota(I32, (FEAT, SEQ), 0) // DK
    head_lanes = lax.broadcasted_iota(I32, (SEQ, FEAT), 1) // DK
    ROWS = 64

    def forward(h):
        mine = jnp.where(head_rows == h, qt_s[...].astype(F32), 0.0).astype(BF)
        s_s[...] = jnp.dot(k_ref[...], mine, preferred_element_type=F32)

        def tile(t, carry):
            lanes = pl.ds(pl.multiple_of(t * 128, 128), 128)
            here = lax.broadcasted_iota(I32, (1, 128), 1) + t * 128
            seg_here = segments(here)
            word_here = here * jnp.int32(668265263) + ka_ref[h, 0] * jnp.int32(-1640531535)
            top = jnp.full((ROWS, 128), -1e30, F32)
            for r in range(0, SEQ, ROWS):
                rows = pl.ds(r, ROWS)
                got = jnp.where(seg_s[rows, :] == seg_here, s_s[rows, lanes], -1e30)
                s_s[rows, lanes] = got
                top = jnp.maximum(top, got)
            top = jnp.max(top, axis=0, keepdims=True)
            mass = jnp.zeros((ROWS, 128), F32)
            for r in range(0, SEQ, ROWS):
                rows = pl.ds(r, ROWS)
                got = jnp.exp(s_s[rows, lanes] - top)
                s_s[rows, lanes] = got
                mass = mass + got
            scale = DROP_SCALE / jnp.sum(mass, axis=0, keepdims=True)
            for r in range(0, SEQ, ROWS):
                rows = pl.ds(r, ROWS)
                keep = kept_bits(spot_s[rows, :] + word_here)
                got = s_s[rows, lanes] * scale
                sp_s[h, rows, lanes] = jnp.where(keep, got, -got)
                kp_s[h, rows, lanes] = jnp.where(keep, got, 0.0).astype(BF)
            return carry

        lax.fori_loop(0, 4, tile, 0)
        ctxf[pl.ds(h * DK, DK), :] = jnp.dot(vt_s[pl.ds(h * DK, DK), :], kp_s[h], preferred_element_type=F32)

    def backward(h):
        mine = jnp.where(head_rows == h, gt_s[...].astype(F32), 0.0).astype(BF)
        s_s[...] = jnp.dot(v_ref[...], mine, preferred_element_type=F32)
        rows_h = pl.ds(h * DK, DK)
        delta = DROP * jnp.sum(gt_s[rows_h, :].astype(F32) * ctxf[rows_h, :], axis=0, keepdims=True)
        for t in range(4):
            lanes = pl.ds(t * 128, 128)
            for r in range(0, SEQ, ROWS):
                rows = pl.ds(r, ROWS)
                d = jnp.broadcast_to(delta[:, t * 128:(t + 1) * 128], (ROWS, 128))
                got = sp_s[h, rows, lanes]
                gs_s[rows, lanes] = (got * jnp.where(got > 0.0, s_s[rows, lanes] - d, d)).astype(BF)
        gqt_s[rows_h, :] = jnp.dot(kt_s[rows_h, :], gs_s[...], preferred_element_type=F32).astype(BF)
        q_h = jnp.where(head_lanes == h, q_ref[...].astype(F32), 0.0).astype(BF)
        g_h = jnp.where(head_lanes == h, g_s[...].astype(F32), 0.0).astype(BF)
        gk = jnp.dot(gs_s[...], q_h, preferred_element_type=F32)
        gv = jnp.dot(kp_s[h], g_h, preferred_element_type=F32)
        if h == 0:
            gka[...] = gk
            gva[...] = gv
        else:
            gka[...] += gk
            gva[...] += gv

    forward(0)
    ring_start()
    forward(1)
    ring_step(1)
    forward(2)
    y_step(1, 0)
    y_step(-1, 0)
    ring_step(2)
    forward(3)
    ctx[...] = ctxf[...].astype(BF).T
    y_step(1, 1)
    y_step(-1, 1)
    ring_step(3)
    y_step(2, 0)
    y_step(2, 1)
    for dy in range(4):
        for piece in range(2):
            ywait(yblock(dy, 1), piece)

    def share(dx, half):
        block = lax.rem(x + dx + NX, NX) * 2 + half
        return jnp.concatenate(
            [jnp.dot(drt[block, piece], ctx[...], preferred_element_type=F32) for piece in range(2)], axis=0
        )

    hop_s[0] = share(2, 0).astype(BF)
    send(hop_s.at[0], hop_r.at[0], xsend.at[0], xrecv.at[0], xp)
    hop_s[1] = share(2, 1).astype(BF)
    send(hop_s.at[1], hop_r.at[1], xsend.at[1], xrecv.at[1], xm)
    fin_s[0] = share(1, 1).astype(BF)
    send(fin_s.at[0], fin_r.at[0], xsend.at[2], xrecv.at[2], xp)
    fin_s[1] = share(-1, 0).astype(BF)
    send(fin_s.at[1], fin_r.at[1], xsend.at[3], xrecv.at[3], xm)
    own[0] = share(0, 0)
    own[1] = share(0, 1)
    ring_step(4)
    fin_s[2] = share(1, 0).astype(BF)
    fin_s[3] = share(-1, 1).astype(BF)
    arrived(hop_r.at[0], xsend.at[0], xrecv.at[0])
    fin_s[2] = (fin_s[2].astype(F32) + hop_r[0].astype(F32)).astype(BF)
    send(fin_s.at[2], fin_r.at[2], xsend.at[4], xrecv.at[4], xp)
    arrived(hop_r.at[1], xsend.at[1], xrecv.at[1])
    fin_s[3] = (fin_s[3].astype(F32) + hop_r[1].astype(F32)).astype(BF)
    send(fin_s.at[3], fin_r.at[3], xsend.at[5], xrecv.at[5], xm)
    ring_step(5)
    ring_step(6)
    ring_step(7)

    for i in range(4):
        arrived(fin_r.at[i], xsend.at[0], xrecv.at[2 + i])
    lower = own[0] + fin_r[1].astype(F32) + fin_r[2].astype(F32)
    upper = own[1] + fin_r[0].astype(F32) + fin_r[3].astype(F32)
    for group in range(4):
        for member in range(4):
            source, row = (lower, group) if group < 2 else (upper, group - 2)
            row = (row * 4 + member) * DK
            near_s[member, group] = source[row:row + DK].astype(BF)
    for i, j in enumerate((1, 2, 3)):
        send(near_s.at[lax.rem(near + j, NEAR)], near_r.at[near], nsend.at[i], nrecv.at[near], near_peers[i])
    ring_step(8)

    def context_part(block):
        half, piece, row = block // 8, (block // 4) % 2, (block % 4) * DK
        left = jnp.concatenate([wt[block, sub] for sub in range(2)], axis=0)
        right = jnp.concatenate([drt[2 * j + half, piece, pl.ds(row, DK), :] for j in range(NX)], axis=0)
        return jnp.dot(left, right, preferred_element_type=F32)

    acc = context_part(0)
    for block in range(1, NZ):
        acc = acc + context_part(block)
    gt_s[...] = acc.astype(BF)
    g_s[...] = gt_s[...].T
    backward(0)
    for j in (1, 2, 3):
        slot = lax.rem(near + j, NEAR)
        arrived(near_r.at[slot], nsend.at[0], nrecv.at[slot])
    total = near_s[near].astype(F32)
    for j in (1, 2, 3):
        total = total + near_r[lax.rem(near + j, NEAR)].astype(F32)
    far_s[...] = total.astype(BF)
    for i, j in enumerate((1, 2, 3)):
        send(far_s.at[lax.rem(far + j, NEAR)], far_r.at[far], fsend.at[i], frecv.at[far], far_peers[i])
    backward(1)
    backward(2)
    backward(3)
    gq_ref[...] = gqt_s[...].T
    gk_ref[...] = gka[...].astype(BF)
    gv_ref[...] = gva[...].astype(BF)
    for j in (1, 2, 3):
        slot = lax.rem(far + j, NEAR)
        arrived(far_r.at[slot], fsend.at[0], frecv.at[slot])
    total = far_s[far].astype(F32)
    for j in (1, 2, 3):
        total = total + far_r[lax.rem(far + j, NEAR)].astype(F32)
    gw_ref[...] = total
    for copy in pending:
        copy.wait_send()


def shards(query, key, value, cotangent, weight_out, keep_attn, keep_out, doc_lengths):
    vmem, smem = pl.BlockSpec(memory_space=pltpu.VMEM), pl.BlockSpec(memory_space=pltpu.SMEM)
    v, dma = pltpu.VMEM, pltpu.SemaphoreType.DMA
    return pl.pallas_call(
        kernel,
        name="attention_backward",
        out_shape=(
            jax.ShapeDtypeStruct((SEQ, FEAT), BF),
            jax.ShapeDtypeStruct((SEQ, FEAT), BF),
            jax.ShapeDtypeStruct((SEQ, FEAT), BF),
            jax.ShapeDtypeStruct((DK, FEAT), F32),
        ),
        in_specs=[vmem, vmem, vmem, vmem, vmem, smem, vmem, smem],
        out_specs=(vmem, vmem, vmem, vmem),
        scratch_shapes=[
            v((8, 2, 256, SEQ), BF),
            v((NX, DK, FEAT), BF),
            v((NZ, 2, 128, FEAT), BF),
            v((FEAT, SEQ), BF),
            v((FEAT, SEQ), BF),
            v((FEAT, SEQ), BF),
            v((FEAT, SEQ), BF),
            v((SEQ, FEAT), BF),
            v((FEAT, SEQ), F32),
            v((SEQ, FEAT), BF),
            v((SEQ, 128), I32),
            v((SEQ, 128), I32),
            v((SEQ, SEQ), F32),
            v((HEADS, SEQ, SEQ), F32),
            v((HEADS, SEQ, SEQ), BF),
            v((SEQ, SEQ), BF),
            v((FEAT, SEQ), BF),
            v((SEQ, FEAT), F32),
            v((SEQ, FEAT), F32),
            v((2, SEQ, FEAT), BF),
            v((2, SEQ, FEAT), BF),
            v((4, SEQ, FEAT), BF),
            v((4, SEQ, FEAT), BF),
            v((2, SEQ, FEAT), F32),
            v((4, 4, DK, FEAT), BF),
            v((4, 4, DK, FEAT), BF),
            v((4, DK, FEAT), BF),
            v((4, DK, FEAT), BF),
            dma((14,)), dma((8, 2)),
            dma((3,)), dma((NX,)),
            dma((32,)), dma((NZ, 2)),
            dma((6,)), dma((6,)),
            dma((3,)), dma((4,)),
            dma((3,)), dma((4,)),
        ],
        compiler_params=pltpu.CompilerParams(
            collective_id=0, has_side_effects=True, vmem_limit_bytes=48 * 2**20
        ),
    )(query, key, value, cotangent, weight_out, keep_attn, keep_out, doc_lengths)


def solution(mesh):
    in_specs = (
        P("dp", "mp"),
        P("dp", "mp"),
        P("dp", "mp"),
        P("dp", "mp"),
        P("dp", "mp"),
        P("mp", "dp"),
        P("dp", "mp"),
        P("dp", None),
    )
    out_specs = (P("dp", "mp"), P("dp", "mp"), P("dp", "mp"), P("dp", "mp"))
    return jax.shard_map(shards, mesh=mesh, in_specs=in_specs, out_specs=out_specs, check_vma=False)
```

```python
import jax
import jax.numpy as jnp
from jax import lax
from jax.experimental import pallas as pl
from jax.experimental.pallas import tpu as pltpu
from jax.sharding import PartitionSpec as P

MESH = pl.DeviceIdType.MESH
BF = jnp.bfloat16
F32 = jnp.float32
I32 = jnp.int32
DK = 64
SEQ = 512
HEADS = 4
FEAT = 256
NX, NY, NZ, NEAR = 4, 4, 16, 4
PIECES = 4
DROP = 0.9
DROP_SCALE = 1.0 / 0.9
TENTH = 429496730
TURN = -1717986918 + 1000
NINE = -(1 << 31) + 200000000


def kept_bits(x):
    x = x ^ lax.shift_right_logical(x, jnp.int32(16))
    x = x * jnp.int32(73244475)
    x = x ^ lax.shift_right_logical(x, jnp.int32(15))
    x = x * jnp.int32(-2048144789)
    x = x ^ lax.shift_right_logical(x, jnp.int32(16))
    return (x & jnp.int32(65535)) * jnp.int32(TENTH) + jnp.int32(TURN) >= jnp.int32(NINE)


def kernel(
    q_hbm, k_hbm, v_hbm, cot_hbm, w_hbm, ka_hbm, ko_hbm, dl_hbm,
    gq_ref, gk_ref, gv_ref, gw_ref,
    q_ref, k_ref, v_ref, cot_ref, w_ref, ka_ref, ko_ref, dl_ref,
    drt, wx, wt, qt_s, kt_s, vt_s, gt_s, g_s, ctxf, ctx, seg_s, spot_s, s_s, sp_s, kp_s, gs_s, gqt_s, gka, gva,
    shr, hop_r, fin_s, fin_r, near_s, near_r, far_s, far_r,
    load, ysend, yrecv, wxsend, wxrecv, wsend, wrecv, xsend, xrecv, nsend, nrecv, fsend, frecv,
):
    dp, mp = lax.axis_index("dp"), lax.axis_index("mp")
    x, z = dp // NZ, lax.rem(dp, NZ)
    y, c = mp // 2, lax.rem(mp, 2)
    near, far = lax.rem(z, NEAR), z // NEAR

    def at(dx=0, dy=0, dz=0, dc=0):
        px, py = lax.rem(x + dx + NX, NX), lax.rem(y + dy + NY, NY)
        pz, pc = lax.rem(z + dz + NZ, NZ), lax.rem(c + dc, 2)
        return (px * NZ + pz, py * 2 + pc)

    def near_peer(j):
        return (x * NZ + far * NEAR + lax.rem(near + j, NEAR), mp)

    core, yp, ym = at(dc=1), at(dy=1), at(dy=-1)
    xp, xm, x2, zp, zm = at(dx=1), at(dx=-1), at(dx=2), at(dz=1), at(dz=-1)
    near_peers = [near_peer(j) for j in range(1, NEAR)]
    greeted = [core, yp, ym, xp, xm, x2, zp, zm]
    barrier = pltpu.get_barrier_semaphore()
    for peer in greeted:
        pl.semaphore_signal(barrier, inc=1, device_id=peer, device_id_type=MESH)

    loads = [
        pltpu.make_async_copy(src, dst, load.at[i])
        for i, (src, dst) in enumerate((
            (ko_hbm, ko_ref), (cot_hbm, cot_ref), (w_hbm, w_ref), (dl_hbm, dl_ref), (ka_hbm, ka_ref),
            (k_hbm, k_ref), (q_hbm, q_ref), (v_hbm, v_ref),
        ))
    ]
    for copy in loads:
        copy.start()

    pending = []

    def send(src, dst, ssem, rsem, peer):
        copy = pltpu.make_async_remote_copy(
            src_ref=src, dst_ref=dst, send_sem=ssem, recv_sem=rsem, device_id=peer, device_id_type=MESH
        )
        copy.start()
        pending.append(copy)

    def arrived(ref, ssem, rsem):
        pltpu.make_async_remote_copy(
            src_ref=ref, dst_ref=ref, send_sem=ssem, recv_sem=rsem, device_id=core, device_id_type=MESH
        ).wait_recv()

    spots = lax.broadcasted_iota(I32, (SEQ, 128), 0)
    first = spots * jnp.int32(668265263)
    for copy in loads[:3]:
        copy.wait()
    for j in range(PIECES):
        lanes = pl.ds(j * 128, 128)
        word = first + ko_ref[:, lanes] * jnp.int32(-1640531535)
        part = jnp.where(kept_bits(word), cot_ref[:, lanes].astype(F32) * DROP_SCALE, 0.0).astype(BF)
        drt[mp, j] = part.T
    wx[x] = w_ref[...]

    pl.semaphore_wait(barrier, len(greeted))

    ysends = [0]

    def ysend_to(block, piece, peer):
        ref = drt.at[block, piece]
        send(ref, ref, ysend.at[ysends[0]], yrecv.at[block, piece], peer)
        ysends[0] += 1

    for i in range(PIECES):
        ysend_to(mp, i, yp)
        ysend_to(mp, (i + 2) % PIECES, ym)
    for i, peer in enumerate((xp, xm, x2)):
        send(wx.at[x], wx.at[x], wxsend.at[i], wxrecv.at[x], peer)
    for i in range(PIECES):
        ysend_to(mp, i, core)

    def yblock(dy, dc=0):
        return lax.rem(y + dy + NY, NY) * 2 + lax.rem(c + dc, 2)

    def ywait(block, piece):
        arrived(drt.at[block, piece], ysend.at[0], yrecv.at[block, piece])

    def y_step(dy, piece):
        block = yblock(dy)
        ywait(block, piece)
        if dy == -1 and piece < 2:
            ysend_to(block, piece, yp)
        if dy == 1 and piece >= 2:
            ysend_to(block, piece, ym)
        ysend_to(block, piece, core)

    wsends = [0]

    def ring_send(block, sub, peer):
        ref = wt.at[block, sub]
        send(ref, ref, wsend.at[wsends[0]], wrecv.at[block, sub], peer)
        wsends[0] += 1

    def ring_start():
        for j in (1, 2, 3):
            block = lax.rem(x + j, NX)
            arrived(wx.at[block], wxsend.at[0], wxrecv.at[block])
        own_w = jnp.concatenate([wx[j] for j in range(NX)], axis=0).T
        for sub in range(2):
            wt[z, sub] = own_w[sub * 128:(sub + 1) * 128]
            ring_send(z, sub, zp)
            ring_send(z, sub, zm)

    def ring_step(k):
        for sub in range(2):
            block = lax.rem(z - k + NZ, NZ)
            arrived(wt.at[block, sub], wsend.at[0], wrecv.at[block, sub])
            if k < NZ // 2:
                ring_send(block, sub, zp)
            if k < NZ // 2:
                block = lax.rem(z + k, NZ)
                arrived(wt.at[block, sub], wsend.at[0], wrecv.at[block, sub])
                if k < NZ // 2 - 1:
                    ring_send(block, sub, zm)

    for copy in loads[3:]:
        copy.wait()
    ends, total = [], 0
    for j in range(8):
        total = total + dl_ref[0, j]
        ends.append(total)

    def segments(places):
        seg = jnp.zeros(places.shape, I32)
        for end in ends:
            seg = seg + (places >= end).astype(I32)
        return seg

    seg_s[...] = segments(spots)
    spot_s[...] = spots * jnp.int32(374761393)
    qt_s[...] = q_ref[...].T
    kt_s[...] = k_ref[...].T
    vt_s[...] = v_ref[...].T
    head_rows = lax.broadcasted_iota(I32, (FEAT, SEQ), 0) // DK
    head_lanes = lax.broadcasted_iota(I32, (SEQ, FEAT), 1) // DK
    ROWS = 64

    def forward(h):
        mine = jnp.where(head_rows == h, qt_s[...].astype(F32), 0.0).astype(BF)
        s_s[...] = jnp.dot(k_ref[...], mine, preferred_element_type=F32)

        def tile(t, carry):
            lanes = pl.ds(pl.multiple_of(t * 128, 128), 128)
            here = lax.broadcasted_iota(I32, (1, 128), 1) + t * 128
            seg_here = segments(here)
            word_here = here * jnp.int32(668265263) + ka_ref[0, h] * jnp.int32(-1640531535)
            top = jnp.full((ROWS, 128), -1e30, F32)
            for r in range(0, SEQ, ROWS):
                rows = pl.ds(r, ROWS)
                got = jnp.where(seg_s[rows, :] == seg_here, s_s[rows, lanes], -1e30)
                s_s[rows, lanes] = got
                top = jnp.maximum(top, got)
            top = jnp.max(top, axis=0, keepdims=True)
            mass = jnp.zeros((ROWS, 128), F32)
            for r in range(0, SEQ, ROWS):
                rows = pl.ds(r, ROWS)
                got = jnp.exp(s_s[rows, lanes] - top)
                s_s[rows, lanes] = got
                mass = mass + got
            scale = DROP_SCALE / jnp.sum(mass, axis=0, keepdims=True)
            for r in range(0, SEQ, ROWS):
                rows = pl.ds(r, ROWS)
                keep = kept_bits(spot_s[rows, :] + word_here)
                got = s_s[rows, lanes] * scale
                sp_s[h, rows, lanes] = jnp.where(keep, got, -got)
                kp_s[h, rows, lanes] = jnp.where(keep, got, 0.0).astype(BF)
            return carry

        lax.fori_loop(0, 4, tile, 0)
        ctxf[pl.ds(h * DK, DK), :] = jnp.dot(vt_s[pl.ds(h * DK, DK), :], kp_s[h], preferred_element_type=F32)

    def backward(h):
        mine = jnp.where(head_rows == h, gt_s[...].astype(F32), 0.0).astype(BF)
        s_s[...] = jnp.dot(v_ref[...], mine, preferred_element_type=F32)
        rows_h = pl.ds(h * DK, DK)
        delta = DROP * jnp.sum(gt_s[rows_h, :].astype(F32) * ctxf[rows_h, :], axis=0, keepdims=True)
        for t in range(4):
            lanes = pl.ds(t * 128, 128)
            for r in range(0, SEQ, ROWS):
                rows = pl.ds(r, ROWS)
                d = jnp.broadcast_to(delta[:, t * 128:(t + 1) * 128], (ROWS, 128))
                got = sp_s[h, rows, lanes]
                gs_s[rows, lanes] = (got * jnp.where(got > 0.0, s_s[rows, lanes] - d, d)).astype(BF)
        gqt_s[rows_h, :] = jnp.dot(kt_s[rows_h, :], gs_s[...], preferred_element_type=F32).astype(BF)
        q_h = jnp.where(head_lanes == h, q_ref[...].astype(F32), 0.0).astype(BF)
        g_h = jnp.where(head_lanes == h, g_s[...].astype(F32), 0.0).astype(BF)
        gk = jnp.dot(gs_s[...], q_h, preferred_element_type=F32)
        gv = jnp.dot(kp_s[h], g_h, preferred_element_type=F32)
        if h == 0:
            gka[...] = gk
            gva[...] = gv
        else:
            gka[...] += gk
            gva[...] += gv

    def dispatch(dy):
        to = lax.rem(y + dy + NY, NY)
        for piece in range(PIECES):
            ywait(yblock(dy, 1), piece)
        for half in range(2):
            for piece in range(PIECES):
                got = jnp.dot(drt[to * 2 + half, piece], ctx[...], preferred_element_type=F32)
                shr[to, half, pl.ds(piece * 128, 128), :] = got.astype(BF)
        dx = lax.rem(to - x + NX, NX)

        @pl.when(dx == 2)
        def _():
            for u in range(2):
                for copy in hop_copies(u):
                    copy.start()

        @pl.when(dx == 1)
        def _():
            for u in range(2):
                early_copy(0, u).start()

        @pl.when(dx == 3)
        def _():
            for u in range(2):
                early_copy(1, u).start()

    def x_copy(src, dst, slot, peer):
        return pltpu.make_async_remote_copy(
            src_ref=src, dst_ref=dst, send_sem=xsend.at[slot], recv_sem=xrecv.at[slot],
            device_id=peer, device_id_type=MESH,
        )

    def part_of(dx, half, u):
        return shr.at[lax.rem(x + dx + NX, NX), half, pl.ds(u * 256, 256)]

    def hop_copies(u):
        return (
            x_copy(part_of(2, 0, u), hop_r.at[0, u], u, xp),
            x_copy(part_of(2, 1, u), hop_r.at[1, u], 2 + u, xm),
        )

    def early_copy(side, u):
        if side == 0:
            return x_copy(part_of(1, 1, u), fin_r.at[0, u], 4 + u, xp)
        return x_copy(part_of(-1, 0, u), fin_r.at[1, u], 6 + u, xm)

    def late_copy(side, u):
        return x_copy(fin_s.at[side, u], fin_r.at[2 + side, u], 8 + 2 * side + u, (xp, xm)[side])

    def hop_step(u):
        for side, copy in enumerate(hop_copies(u)):
            copy.wait_recv()
            mine = part_of((1, -1)[side], side, u)
            fin_s[side, u] = (mine[...].astype(F32) + hop_r[side, u].astype(F32)).astype(BF)
            late_copy(side, u).start()

    def near_copy(group, i):
        j = i + 1
        return pltpu.make_async_remote_copy(
            src_ref=near_s.at[group, lax.rem(near + j, NEAR)], dst_ref=near_r.at[group, near],
            send_sem=nsend.at[group, i], recv_sem=nrecv.at[group, near], device_id=near_peers[i], device_id_type=MESH,
        )

    def fin_step(half, u):
        group = 2 * half + u
        early_copy(1 - half, u).wait_recv()
        late_copy(half, u).wait_recv()
        total = part_of(0, half, u)[...].astype(F32)
        total = total + fin_r[1 - half, u].astype(F32) + fin_r[2 + half, u].astype(F32)
        near_s[group] = total.astype(BF).reshape(NEAR, DK, FEAT)
        for i in range(NEAR - 1):
            near_copy(group, i).start()

    def far_copy(group):
        return pltpu.make_async_remote_copy(
            src_ref=far_s.at[group], dst_ref=far_r.at[far], send_sem=fsend.at[group], recv_sem=frecv.at[far],
            device_id=(x * NZ + group * NEAR + near, mp), device_id_type=MESH,
        )

    def near_step(group):
        total = near_s[group, near].astype(F32)
        for j in range(1, NEAR):
            slot = lax.rem(near + j, NEAR)
            arrived(near_r.at[group, slot], nsend.at[0, 0], nrecv.at[group, slot])
            total = total + near_r[group, slot].astype(F32)
        far_s[group] = total.astype(BF)

        @pl.when(far != group)
        def _():
            far_copy(group).start()

    def context_part(block):
        half, piece, row = block // 8, (block % 8) // 2, (block % 2) * DK
        left = jnp.concatenate([wt[block, sub] for sub in range(2)], axis=0)
        right = jnp.concatenate([drt[2 * j + half, piece, pl.ds(row, DK), :] for j in range(NX)], axis=0)
        return jnp.dot(left, right, preferred_element_type=F32)

    forward(0)
    ring_start()
    forward(1)
    y_step(-1, 0)
    y_step(1, 2)
    ring_step(1)
    forward(2)
    y_step(-1, 1)
    y_step(1, 3)
    ring_step(2)
    forward(3)
    ctx[...] = ctxf[...].astype(BF).T
    y_step(-1, 2)
    y_step(1, 0)
    dispatch(0)
    ring_step(3)
    y_step(-1, 3)
    y_step(1, 1)
    dispatch(1)
    dispatch(-1)
    ring_step(4)
    for piece in (0, 2, 1, 3):
        y_step(2, piece)
    ring_step(5)
    dispatch(2)
    hop_step(0)
    ring_step(6)
    hop_step(1)
    ring_step(7)
    fin_step(0, 0)
    fin_step(1, 0)
    ring_step(8)
    fin_step(0, 1)
    fin_step(1, 1)
    acc = context_part(0)
    for block in range(1, NZ):
        acc = acc + context_part(block)
    gt_s[...] = acc.astype(BF)
    near_step(0)
    near_step(2)
    near_step(1)
    near_step(3)
    g_s[...] = gt_s[...].T
    for h in range(HEADS):
        backward(h)
    gq_ref[...] = gqt_s[...].T
    gk_ref[...] = gka[...].astype(BF)
    gv_ref[...] = gva[...].astype(BF)
    total = far_s[far].astype(F32)
    for j in range(1, NEAR):
        slot = lax.rem(far + j, NEAR)
        arrived(far_r.at[slot], fsend.at[0], frecv.at[slot])
        total = total + far_r[slot].astype(F32)
    gw_ref[...] = total
    for copy in pending:
        copy.wait_send()
    for u in range(2):
        for copy in hop_copies(u):
            copy.wait_send()
        for side in range(2):
            early_copy(side, u).wait_send()
            late_copy(side, u).wait_send()
    for group in range(NEAR):
        for i in range(NEAR - 1):
            near_copy(group, i).wait_send()

        @pl.when(far != group)
        def _(group=group):
            far_copy(group).wait_send()


def shards(query, key, value, cotangent, weight_out, keep_attn, keep_out, doc_lengths):
    vmem, hbm = pl.BlockSpec(memory_space=pltpu.VMEM), pl.BlockSpec(memory_space=pltpu.HBM)
    v, dma = pltpu.VMEM, pltpu.SemaphoreType.DMA
    return pl.pallas_call(
        kernel,
        name="attention_backward",
        out_shape=(
            jax.ShapeDtypeStruct((SEQ, FEAT), BF),
            jax.ShapeDtypeStruct((SEQ, FEAT), BF),
            jax.ShapeDtypeStruct((SEQ, FEAT), BF),
            jax.ShapeDtypeStruct((DK, FEAT), F32),
        ),
        in_specs=[hbm] * 8,
        out_specs=(vmem, vmem, vmem, vmem),
        scratch_shapes=[
            v((SEQ, FEAT), BF),
            v((SEQ, FEAT), BF),
            v((SEQ, FEAT), BF),
            v((SEQ, SEQ), BF),
            v((DK, FEAT), BF),
            pltpu.SMEM((1, HEADS), I32),
            v((1, SEQ), I32),
            pltpu.SMEM((1, 8), I32),
            v((8, PIECES, 128, SEQ), BF),
            v((NX, DK, FEAT), BF),
            v((NZ, 2, 128, FEAT), BF),
            v((FEAT, SEQ), BF),
            v((FEAT, SEQ), BF),
            v((FEAT, SEQ), BF),
            v((FEAT, SEQ), BF),
            v((SEQ, FEAT), BF),
            v((FEAT, SEQ), F32),
            v((SEQ, FEAT), BF),
            v((SEQ, 128), I32),
            v((SEQ, 128), I32),
            v((SEQ, SEQ), F32),
            v((HEADS, SEQ, SEQ), F32),
            v((HEADS, SEQ, SEQ), BF),
            v((SEQ, SEQ), BF),
            v((FEAT, SEQ), BF),
            v((SEQ, FEAT), F32),
            v((SEQ, FEAT), F32),
            v((NX, 2, SEQ, FEAT), BF),
            v((2, 2, 256, FEAT), BF),
            v((2, 2, 256, FEAT), BF),
            v((4, 2, 256, FEAT), BF),
            v((4, NEAR, DK, FEAT), BF),
            v((4, NEAR, DK, FEAT), BF),
            v((4, DK, FEAT), BF),
            v((4, DK, FEAT), BF),
            dma((8,)),
            dma((28,)), dma((8, PIECES)),
            dma((3,)), dma((NX,)),
            dma((32,)), dma((NZ, 2)),
            dma((12,)), dma((12,)),
            dma((4, 3)), dma((4, NEAR)),
            dma((4,)), dma((4,)),
        ],
        compiler_params=pltpu.CompilerParams(
            collective_id=0, has_side_effects=True, vmem_limit_bytes=60 * 2**20
        ),
    )(query, key, value, cotangent, weight_out, keep_attn.reshape(1, HEADS), keep_out, doc_lengths)


def solution(mesh):
    in_specs = (
        P("dp", "mp"),
        P("dp", "mp"),
        P("dp", "mp"),
        P("dp", "mp"),
        P("dp", "mp"),
        P("mp", "dp"),
        P("dp", "mp"),
        P("dp", None),
    )
    out_specs = (P("dp", "mp"), P("dp", "mp"), P("dp", "mp"), P("dp", "mp"))
    return jax.shard_map(shards, mesh=mesh, in_specs=in_specs, out_specs=out_specs, check_vma=False)
```

```python
import jax
import jax.numpy as jnp
from jax import lax
from jax.experimental import pallas as pl
from jax.experimental.pallas import tpu as pltpu
from jax.sharding import PartitionSpec as P

MESH = pl.DeviceIdType.MESH
BF = jnp.bfloat16
F32 = jnp.float32
I32 = jnp.int32
DK = 64
SEQ = 512
HEADS = 4
FEAT = 256
NX, NY, NZ, NEAR = 4, 4, 16, 4
PIECES = 4
DROP = 0.9
DROP_SCALE = 1.0 / 0.9
TENTH = 429496730
TURN = -1717986918 + 1000
NINE = -(1 << 31) + 200000000


def kept_bits(x):
    x = x ^ lax.shift_right_logical(x, jnp.int32(16))
    x = x * jnp.int32(73244475)
    x = x ^ lax.shift_right_logical(x, jnp.int32(15))
    x = x * jnp.int32(-2048144789)
    x = x ^ lax.shift_right_logical(x, jnp.int32(16))
    return (x & jnp.int32(65535)) * jnp.int32(TENTH) + jnp.int32(TURN) >= jnp.int32(NINE)


def kernel(
    q_hbm, k_hbm, v_hbm, cot_hbm, w_hbm, ka_hbm, ko_hbm, dl_hbm,
    gq_hbm, gk_hbm, gv_hbm, gw_hbm,
    q_ref, k_ref, v_ref, cot_ref, w_ref, ka_ref, ko_ref, dl_ref,
    drt, wx, wt, qt_s, kt_s, vt_s, gt_s, g_s, ctxf, ctx, seg_s, spot_s, s_s, sp_s, kp_s, gs_s, gqt_s, gka, gva,
    shr, hop_r, fin_s, fin_r, near_s, near_r, far_s, far_r,
    gq_ref, gk_ref, gv_ref, gw_ref, load, store, ysend, yrecv, wxsend, wxrecv, wsend, wrecv, xsend, xrecv, nsend, nrecv, fsend, frecv,
):
    dp, mp = lax.axis_index("dp"), lax.axis_index("mp")
    x, z = dp // NZ, lax.rem(dp, NZ)
    y, c = mp // 2, lax.rem(mp, 2)
    near, far = lax.rem(z, NEAR), z // NEAR
    role = lax.rem(y - x + NX, NX)

    def at(dx=0, dy=0, dz=0, dc=0):
        px, py = lax.rem(x + dx + NX, NX), lax.rem(y + dy + NY, NY)
        pz, pc = lax.rem(z + dz + NZ, NZ), lax.rem(c + dc, 2)
        return (px * NZ + pz, py * 2 + pc)

    def near_peer(j):
        return (x * NZ + far * NEAR + lax.rem(near + j, NEAR), mp)

    core, yp, ym = at(dc=1), at(dy=1), at(dy=-1)
    xp, xm, x2, zp, zm = at(dx=1), at(dx=-1), at(dx=2), at(dz=1), at(dz=-1)
    near_peers = [near_peer(j) for j in range(1, NEAR)]
    greeted = [core, yp, ym, xp, xm, x2, zp, zm]
    barrier = pltpu.get_barrier_semaphore()
    for peer in greeted:
        pl.semaphore_signal(barrier, inc=1, device_id=peer, device_id_type=MESH)

    loads = [
        pltpu.make_async_copy(src, dst, load.at[i])
        for i, (src, dst) in enumerate((
            (ko_hbm, ko_ref), (cot_hbm, cot_ref), (w_hbm, w_ref), (dl_hbm, dl_ref), (ka_hbm, ka_ref),
            (k_hbm, k_ref), (q_hbm, q_ref), (v_hbm, v_ref),
        ))
    ]
    for copy in loads:
        copy.start()

    pending = []

    def send(src, dst, ssem, rsem, peer):
        copy = pltpu.make_async_remote_copy(
            src_ref=src, dst_ref=dst, send_sem=ssem, recv_sem=rsem, device_id=peer, device_id_type=MESH
        )
        copy.start()
        pending.append(copy)

    def arrived(ref, ssem, rsem):
        pltpu.make_async_remote_copy(
            src_ref=ref, dst_ref=ref, send_sem=ssem, recv_sem=rsem, device_id=core, device_id_type=MESH
        ).wait_recv()

    spots = lax.broadcasted_iota(I32, (SEQ, 128), 0)
    first = spots * jnp.int32(668265263)
    for copy in loads[:3]:
        copy.wait()
    for j in range(PIECES):
        lanes = pl.ds(j * 128, 128)
        word = first + ko_ref[:, lanes] * jnp.int32(-1640531535)
        part = jnp.where(kept_bits(word), cot_ref[:, lanes].astype(F32) * DROP_SCALE, 0.0).astype(BF)
        drt[mp, j] = part.T
    wx[x] = w_ref[...]

    pl.semaphore_wait(barrier, len(greeted))

    ysends = [0]

    def ysend_to(block, piece, peer):
        ref = drt.at[block, piece]
        send(ref, ref, ysend.at[ysends[0]], yrecv.at[block, piece], peer)
        ysends[0] += 1

    def ysend_own(first):
        for i in range(2):
            ysend_to(mp, i if first else 2 + i, yp)
            ysend_to(mp, 2 + i if first else i, ym)

    ysend_own(True)
    for i, peer in enumerate((xp, xm, x2)):
        send(wx.at[x], wx.at[x], wxsend.at[i], wxrecv.at[x], peer)
    for i in range(PIECES):
        ysend_to(mp, i, core)

    def yblock(dy, dc=0):
        return lax.rem(y + dy + NY, NY) * 2 + lax.rem(c + dc, 2)

    def ywait(block, piece):
        arrived(drt.at[block, piece], ysend.at[0], yrecv.at[block, piece])

    def y_step(dy, piece):
        block = yblock(dy)
        ywait(block, piece)
        if dy == -1 and piece < 2:
            ysend_to(block, piece, yp)
        if dy == 1 and piece >= 2:
            ysend_to(block, piece, ym)
        ysend_to(block, piece, core)

    wsends = [0]

    def ring_send(block, sub, peer):
        ref = wt.at[block, sub]
        send(ref, ref, wsend.at[wsends[0]], wrecv.at[block, sub], peer)
        wsends[0] += 1

    def ring_start():
        for j in (1, 2, 3):
            block = lax.rem(x + j, NX)
            arrived(wx.at[block], wxsend.at[0], wxrecv.at[block])
        own_w = jnp.concatenate([wx[j] for j in range(NX)], axis=0).T
        for sub in range(2):
            wt[z, sub] = own_w[sub * 128:(sub + 1) * 128]
            ring_send(z, sub, zp)
            ring_send(z, sub, zm)

    def ring_step(k):
        for sub in range(2):
            block = lax.rem(z - k + NZ, NZ)
            arrived(wt.at[block, sub], wsend.at[0], wrecv.at[block, sub])
            if k < NZ // 2:
                ring_send(block, sub, zp)
            if k < NZ // 2:
                block = lax.rem(z + k, NZ)
                arrived(wt.at[block, sub], wsend.at[0], wrecv.at[block, sub])
                if k < NZ // 2 - 1:
                    ring_send(block, sub, zm)

    for copy in loads[3:]:
        copy.wait()
    ends, total = [], 0
    for j in range(8):
        total = total + dl_ref[0, j]
        ends.append(total)

    def segments(places):
        seg = jnp.zeros(places.shape, I32)
        for end in ends:
            seg = seg + (places >= end).astype(I32)
        return seg

    seg_s[...] = segments(spots)
    spot_s[...] = spots * jnp.int32(374761393)
    qt_s[...] = q_ref[...].T
    kt_s[...] = k_ref[...].T
    vt_s[...] = v_ref[...].T
    head_rows = lax.broadcasted_iota(I32, (FEAT, SEQ), 0) // DK
    head_lanes = lax.broadcasted_iota(I32, (SEQ, FEAT), 1) // DK
    ROWS = 64

    def forward(h):
        mine = jnp.where(head_rows == h, qt_s[...].astype(F32), 0.0).astype(BF)
        s_s[...] = jnp.dot(k_ref[...], mine, preferred_element_type=F32)

        def tile(t, carry):
            lanes = pl.ds(pl.multiple_of(t * 128, 128), 128)
            here = lax.broadcasted_iota(I32, (1, 128), 1) + t * 128
            seg_here = segments(here)
            word_here = here * jnp.int32(668265263) + ka_ref[0, h] * jnp.int32(-1640531535)
            top = jnp.full((ROWS, 128), -1e30, F32)
            for r in range(0, SEQ, ROWS):
                rows = pl.ds(r, ROWS)
                got = jnp.where(seg_s[rows, :] == seg_here, s_s[rows, lanes], -1e30)
                s_s[rows, lanes] = got
                top = jnp.maximum(top, got)
            top = jnp.max(top, axis=0, keepdims=True)
            mass = jnp.zeros((ROWS, 128), F32)
            for r in range(0, SEQ, ROWS):
                rows = pl.ds(r, ROWS)
                got = jnp.exp(s_s[rows, lanes] - top)
                s_s[rows, lanes] = got
                mass = mass + got
            scale = DROP_SCALE / jnp.sum(mass, axis=0, keepdims=True)
            for r in range(0, SEQ, ROWS):
                rows = pl.ds(r, ROWS)
                keep = kept_bits(spot_s[rows, :] + word_here)
                got = s_s[rows, lanes] * scale
                sp_s[h, rows, lanes] = jnp.where(keep, got, -got)
                kp_s[h, rows, lanes] = jnp.where(keep, got, 0.0).astype(BF)
            return carry

        lax.fori_loop(0, 4, tile, 0)
        ctxf[pl.ds(h * DK, DK), :] = jnp.dot(vt_s[pl.ds(h * DK, DK), :], kp_s[h], preferred_element_type=F32)

    def backward(h):
        mine = jnp.where(head_rows == h, gt_s[...].astype(F32), 0.0).astype(BF)
        s_s[...] = jnp.dot(v_ref[...], mine, preferred_element_type=F32)
        rows_h = pl.ds(h * DK, DK)
        delta = DROP * jnp.sum(gt_s[rows_h, :].astype(F32) * ctxf[rows_h, :], axis=0, keepdims=True)
        for t in range(4):
            lanes = pl.ds(t * 128, 128)
            for r in range(0, SEQ, ROWS):
                rows = pl.ds(r, ROWS)
                d = jnp.broadcast_to(delta[:, t * 128:(t + 1) * 128], (ROWS, 128))
                got = sp_s[h, rows, lanes]
                gs_s[rows, lanes] = (got * jnp.where(got > 0.0, s_s[rows, lanes] - d, d)).astype(BF)
        gqt_s[rows_h, :] = jnp.dot(kt_s[rows_h, :], gs_s[...], preferred_element_type=F32).astype(BF)
        q_h = jnp.where(head_lanes == h, q_ref[...].astype(F32), 0.0).astype(BF)
        g_h = jnp.where(head_lanes == h, g_s[...].astype(F32), 0.0).astype(BF)
        gk = jnp.dot(gs_s[...], q_h, preferred_element_type=F32)
        gv = jnp.dot(kp_s[h], g_h, preferred_element_type=F32)
        if h == 0:
            gka[...] = gk
            gva[...] = gv
        else:
            gka[...] += gk
            gva[...] += gv

    def dispatch(dy, u):
        to = lax.rem(y + dy + NY, NY)
        for piece in (2 * u, 2 * u + 1):
            ywait(yblock(dy, 1), piece)
        for half in range(2):
            for piece in (2 * u, 2 * u + 1):
                got = jnp.dot(drt[to * 2 + half, piece], ctx[...], preferred_element_type=F32)
                shr[to, half, pl.ds(piece * 128, 128), :] = got.astype(BF)
        dx = lax.rem(to - x + NX, NX)

        @pl.when(dx == 2)
        def _():
            for side in range(2):
                hop_copy(side, u).start()

        @pl.when(dx == 1)
        def _():
            early_copy(0, u).start()

        @pl.when(dx == 3)
        def _():
            early_copy(1, u).start()

    def x_copy(src, dst, slot, peer):
        return pltpu.make_async_remote_copy(
            src_ref=src, dst_ref=dst, send_sem=xsend.at[slot], recv_sem=xrecv.at[slot],
            device_id=peer, device_id_type=MESH,
        )

    def part_of(dx, half, u):
        return shr.at[lax.rem(x + dx + NX, NX), half, pl.ds(u * 256 if isinstance(u, int) else pl.multiple_of(u * 256, 256), 256)]

    def hop_copy(side, u):
        return x_copy(part_of(2, side, u), hop_r.at[side, u], 2 * side + u, (xp, xm)[side])

    def early_copy(side, u):
        if side == 0:
            return x_copy(part_of(1, 1, u), fin_r.at[0, u], 4 + u, xp)
        return x_copy(part_of(-1, 0, u), fin_r.at[1, u], 6 + u, xm)

    def late_copy(side, u):
        return x_copy(fin_s.at[side, u], fin_r.at[2 + side, u], 8 + 2 * side + u, (xp, xm)[side])

    def hop_step(side, u):
        hop_copy(side, u).wait_recv()
        mine = part_of((1, -1)[side], side, u)
        fin_s[side, u] = (mine[...].astype(F32) + hop_r[side, u].astype(F32)).astype(BF)
        late_copy(side, u).start()

    def near_copy(group, i):
        j = i + 1
        return pltpu.make_async_remote_copy(
            src_ref=near_s.at[group, lax.rem(near + j, NEAR)], dst_ref=near_r.at[group, near],
            send_sem=nsend.at[group, i], recv_sem=nrecv.at[group, near], device_id=near_peers[i], device_id_type=MESH,
        )

    def fin_step(half, u):
        group = 2 * half + u
        early_copy(1 - half, u).wait_recv()
        late_copy(half, u).wait_recv()
        total = part_of(0, half, u)[...].astype(F32)
        total = total + fin_r[1 - half, u].astype(F32) + fin_r[2 + half, u].astype(F32)
        near_s[group] = total.astype(BF).reshape(NEAR, DK, FEAT)
        for i in range(NEAR - 1):
            near_copy(group, i).start()

    def far_copy(group):
        return pltpu.make_async_remote_copy(
            src_ref=far_s.at[group], dst_ref=far_r.at[far], send_sem=fsend.at[group], recv_sem=frecv.at[far],
            device_id=(x * NZ + group * NEAR + near, mp), device_id_type=MESH,
        )

    def near_step(group):
        total = near_s[group, near].astype(F32)
        for j in range(1, NEAR):
            slot = lax.rem(near + j, NEAR)
            arrived(near_r.at[group, slot], nsend.at[0, 0], nrecv.at[group, slot])
            total = total + near_r[group, slot].astype(F32)
        far_s[group] = total.astype(BF)

        @pl.when(far != group)
        def _():
            far_copy(group).start()

    def context_part(block):
        half, piece, row = block // 8, (block % 8) // 2, (block % 2) * DK
        left = jnp.concatenate([wt[block, sub] for sub in range(2)], axis=0)
        right = jnp.concatenate([drt[2 * j + half, piece, pl.ds(row, DK), :] for j in range(NX)], axis=0)
        return jnp.dot(left, right, preferred_element_type=F32)

    forward(0)
    ring_start()
    forward(1)
    y_step(-1, 0)
    y_step(1, 2)
    ring_step(1)
    forward(2)
    y_step(-1, 1)
    y_step(1, 3)
    ysend_to(mp, 2, yp)
    ysend_to(mp, 0, ym)
    forward(3)
    ctx[...] = ctxf[...].astype(BF).T
    ring_step(2)
    dispatch(0, 0)
    dispatch(0, 1)
    dispatch(-1, 0)
    dispatch(1, 1)
    ysend_to(mp, 3, yp)
    ysend_to(mp, 1, ym)
    y_step(2, 0)
    y_step(2, 2)
    ring_step(3)
    y_step(2, 1)
    y_step(2, 3)
    dispatch(2, 0)
    dispatch(2, 1)
    y_step(-1, 2)
    y_step(1, 0)
    ring_step(4)
    y_step(-1, 3)
    y_step(1, 1)
    dispatch(-1, 1)
    dispatch(1, 0)
    ring_step(5)
    hop_first = (jnp.where(role == 2, 0, 1), jnp.where(role == 2, 1, 0))
    fin_first = (jnp.where(role == 1, 0, 1), jnp.where(role == 3, 1, 0))
    for side in range(2):
        hop_step(side, hop_first[side])
    for side in range(2):
        hop_step(side, 1 - hop_first[side])
    ring_step(6)
    for half in range(2):
        fin_step(half, fin_first[half])
    ring_step(7)
    for half in range(2):
        fin_step(half, 1 - fin_first[half])
    ring_step(8)
    acc = context_part(0)
    for block in range(1, NZ):
        acc = acc + context_part(block)
    gt_s[...] = acc.astype(BF)
    for half in range(2):
        near_step(2 * half + fin_first[half])
    for half in range(2):
        near_step(2 * half + 1 - fin_first[half])
    g_s[...] = gt_s[...].T
    for h in range(HEADS):
        backward(h)
    gq_ref[...] = gqt_s[...].T
    gk_ref[...] = gka[...].astype(BF)
    gv_ref[...] = gva[...].astype(BF)
    stores = [
        pltpu.make_async_copy(src, dst, store.at[i])
        for i, (src, dst) in enumerate(((gq_ref, gq_hbm), (gk_ref, gk_hbm), (gv_ref, gv_hbm), (gw_ref, gw_hbm)))
    ]
    for copy in stores[:3]:
        copy.start()
    total = far_s[far].astype(F32)
    for j in range(1, NEAR):
        slot = lax.rem(far + j, NEAR)
        arrived(far_r.at[slot], fsend.at[0], frecv.at[slot])
        total = total + far_r[slot].astype(F32)
    gw_ref[...] = total
    stores[3].start()
    for copy in pending:
        copy.wait_send()
    for copy in stores:
        copy.wait()
    for u in range(2):
        for side in range(2):
            hop_copy(side, u).wait_send()
            early_copy(side, u).wait_send()
            late_copy(side, u).wait_send()
    for group in range(NEAR):
        for i in range(NEAR - 1):
            near_copy(group, i).wait_send()

        @pl.when(far != group)
        def _(group=group):
            far_copy(group).wait_send()


def hand_over(*refs):
    for source, out in zip(refs[:4], refs[4:]):
        out[...] = source[...]


def shards(query, key, value, cotangent, weight_out, keep_attn, keep_out, doc_lengths):
    vmem, hbm = pl.BlockSpec(memory_space=pltpu.VMEM), pl.BlockSpec(memory_space=pltpu.HBM)
    v, dma = pltpu.VMEM, pltpu.SemaphoreType.DMA
    grads = pl.pallas_call(
        kernel,
        name="attention_backward",
        out_shape=(
            jax.ShapeDtypeStruct((SEQ, FEAT), BF),
            jax.ShapeDtypeStruct((SEQ, FEAT), BF),
            jax.ShapeDtypeStruct((SEQ, FEAT), BF),
            jax.ShapeDtypeStruct((DK, FEAT), F32),
        ),
        in_specs=[hbm] * 8,
        out_specs=(hbm,) * 4,
        scratch_shapes=[
            v((SEQ, FEAT), BF),
            v((SEQ, FEAT), BF),
            v((SEQ, FEAT), BF),
            v((SEQ, SEQ), BF),
            v((DK, FEAT), BF),
            pltpu.SMEM((1, HEADS), I32),
            v((1, SEQ), I32),
            pltpu.SMEM((1, 8), I32),
            v((8, PIECES, 128, SEQ), BF),
            v((NX, DK, FEAT), BF),
            v((NZ, 2, 128, FEAT), BF),
            v((FEAT, SEQ), BF),
            v((FEAT, SEQ), BF),
            v((FEAT, SEQ), BF),
            v((FEAT, SEQ), BF),
            v((SEQ, FEAT), BF),
            v((FEAT, SEQ), F32),
            v((SEQ, FEAT), BF),
            v((SEQ, 128), I32),
            v((SEQ, 128), I32),
            v((SEQ, SEQ), F32),
            v((HEADS, SEQ, SEQ), F32),
            v((HEADS, SEQ, SEQ), BF),
            v((SEQ, SEQ), BF),
            v((FEAT, SEQ), BF),
            v((SEQ, FEAT), F32),
            v((SEQ, FEAT), F32),
            v((NX, 2, SEQ, FEAT), BF),
            v((2, 2, 256, FEAT), BF),
            v((2, 2, 256, FEAT), BF),
            v((4, 2, 256, FEAT), BF),
            v((4, NEAR, DK, FEAT), BF),
            v((4, NEAR, DK, FEAT), BF),
            v((4, DK, FEAT), BF),
            v((4, DK, FEAT), BF),
            v((SEQ, FEAT), BF),
            v((SEQ, FEAT), BF),
            v((SEQ, FEAT), BF),
            v((DK, FEAT), F32),
            dma((8,)), dma((4,)),
            dma((28,)), dma((8, PIECES)),
            dma((3,)), dma((NX,)),
            dma((32,)), dma((NZ, 2)),
            dma((12,)), dma((12,)),
            dma((4, 3)), dma((4, NEAR)),
            dma((4,)), dma((4,)),
        ],
        compiler_params=pltpu.CompilerParams(
            collective_id=0, has_side_effects=True, vmem_limit_bytes=60 * 2**20
        ),
    )(query, key, value, cotangent, weight_out, keep_attn.reshape(1, HEADS), keep_out, doc_lengths)
    return pl.pallas_call(
        hand_over,
        name="hand_over",
        out_shape=tuple(jax.ShapeDtypeStruct(g.shape, g.dtype) for g in grads),
        in_specs=[vmem] * 4,
        out_specs=(vmem,) * 4,
        compiler_params=pltpu.CompilerParams(vmem_limit_bytes=60 * 2**20),
    )(*grads)


def solution(mesh):
    in_specs = (
        P("dp", "mp"),
        P("dp", "mp"),
        P("dp", "mp"),
        P("dp", "mp"),
        P("dp", "mp"),
        P("mp", "dp"),
        P("dp", "mp"),
        P("dp", None),
    )
    out_specs = (P("dp", "mp"), P("dp", "mp"), P("dp", "mp"), P("dp", "mp"))
    return jax.shard_map(shards, mesh=mesh, in_specs=in_specs, out_specs=out_specs, check_vma=False)
```

```python
import jax
import jax.numpy as jnp
from jax import lax
from jax.experimental import pallas as pl
from jax.experimental.pallas import tpu as pltpu
from jax.sharding import PartitionSpec as P

MESH = pl.DeviceIdType.MESH
BF = jnp.bfloat16
F32 = jnp.float32
I32 = jnp.int32
DK = 64
SEQ = 512
HEADS = 4
FEAT = 256
NX, NY, NZ, NEAR = 4, 4, 16, 4
PIECES = 4
DROP = 0.9
DROP_SCALE = 1.0 / 0.9
TENTH = 429496730
TURN = -1717986918 + 1000
NINE = -(1 << 31) + 200000000


def kept_bits(x):
    x = x ^ lax.shift_right_logical(x, jnp.int32(16))
    x = x * jnp.int32(73244475)
    x = x ^ lax.shift_right_logical(x, jnp.int32(15))
    x = x * jnp.int32(-2048144789)
    x = x ^ lax.shift_right_logical(x, jnp.int32(16))
    return (x & jnp.int32(65535)) * jnp.int32(TENTH) + jnp.int32(TURN) >= jnp.int32(NINE)


def kernel(
    q_hbm, k_hbm, v_hbm, cot_hbm, w_hbm, ka_hbm, ko_hbm, dl_hbm,
    gq_hbm, gk_hbm, gv_hbm, gw_hbm,
    q_ref, k_ref, v_ref, cot_ref, w_ref, ka_ref, ko_ref, dl_ref,
    drt, wx, wt, qt_s, kt_s, vt_s, gt_s, g_s, ctxf, ctx, seg_s, spot_s, s_s, sp_s, kp_s, gs_s, gqt_s, gka, gva,
    shr, hop_r, fin_s, fin_r, near_s, near_r, far_s, far_r,
    gq_ref, gk_ref, gv_ref, gw_ref, load, store, ysend, yrecv, wxsend, wxrecv, wsend, wrecv, xsend, xrecv, nsend, nrecv, fsend, frecv,
):
    dp, mp = lax.axis_index("dp"), lax.axis_index("mp")
    x, z = dp // NZ, lax.rem(dp, NZ)
    y, c = mp // 2, lax.rem(mp, 2)
    near, far = lax.rem(z, NEAR), z // NEAR
    role = lax.rem(y - x + NX, NX)

    def at(dx=0, dy=0, dz=0, dc=0):
        px, py = lax.rem(x + dx + NX, NX), lax.rem(y + dy + NY, NY)
        pz, pc = lax.rem(z + dz + NZ, NZ), lax.rem(c + dc, 2)
        return (px * NZ + pz, py * 2 + pc)

    def near_peer(j):
        return (x * NZ + far * NEAR + lax.rem(near + j, NEAR), mp)

    core, yp, ym = at(dc=1), at(dy=1), at(dy=-1)
    xp, xm, x2, zp, zm = at(dx=1), at(dx=-1), at(dx=2), at(dz=1), at(dz=-1)
    near_peers = [near_peer(j) for j in range(1, NEAR)]
    greeted = [core, yp, ym, xp, xm, x2, zp, zm]
    barrier = pltpu.get_barrier_semaphore()
    for peer in greeted:
        pl.semaphore_signal(barrier, inc=1, device_id=peer, device_id_type=MESH)

    loads = [
        pltpu.make_async_copy(src, dst, load.at[i])
        for i, (src, dst) in enumerate((
            (ko_hbm, ko_ref), (cot_hbm, cot_ref), (w_hbm, w_ref), (dl_hbm, dl_ref), (ka_hbm, ka_ref),
            (k_hbm, k_ref), (q_hbm, q_ref), (v_hbm, v_ref),
        ))
    ]
    for copy in loads:
        copy.start()

    pending = []

    def send(src, dst, ssem, rsem, peer):
        copy = pltpu.make_async_remote_copy(
            src_ref=src, dst_ref=dst, send_sem=ssem, recv_sem=rsem, device_id=peer, device_id_type=MESH
        )
        copy.start()
        pending.append(copy)

    def arrived(ref, ssem, rsem):
        pltpu.make_async_remote_copy(
            src_ref=ref, dst_ref=ref, send_sem=ssem, recv_sem=rsem, device_id=core, device_id_type=MESH
        ).wait_recv()

    spots = lax.broadcasted_iota(I32, (SEQ, 128), 0)
    first = spots * jnp.int32(668265263)
    for copy in loads[:3]:
        copy.wait()
    for j in range(PIECES):
        lanes = pl.ds(j * 128, 128)
        word = first + ko_ref[:, lanes] * jnp.int32(-1640531535)
        part = jnp.where(kept_bits(word), cot_ref[:, lanes].astype(F32) * DROP_SCALE, 0.0).astype(BF)
        drt[mp, j] = part.T
    wx[x] = w_ref[...]

    pl.semaphore_wait(barrier, len(greeted))

    ysends = [0]

    def ysend_to(block, piece, peer):
        ref = drt.at[block, piece]
        send(ref, ref, ysend.at[ysends[0]], yrecv.at[block, piece], peer)
        ysends[0] += 1

    def ysend_own(first):
        for i in range(2):
            ysend_to(mp, i if first else 2 + i, yp)
            ysend_to(mp, 2 + i if first else i, ym)

    ysend_own(True)
    for i, peer in enumerate((xp, xm, x2)):
        send(wx.at[x], wx.at[x], wxsend.at[i], wxrecv.at[x], peer)
    for i in range(PIECES):
        ysend_to(mp, i, core)

    def yblock(dy, dc=0):
        return lax.rem(y + dy + NY, NY) * 2 + lax.rem(c + dc, 2)

    def ywait(block, piece):
        arrived(drt.at[block, piece], ysend.at[0], yrecv.at[block, piece])

    def y_step(dy, piece):
        block = yblock(dy)
        ywait(block, piece)
        if dy == -1 and piece < 2:
            ysend_to(block, piece, yp)
        if dy == 1 and piece >= 2:
            ysend_to(block, piece, ym)
        ysend_to(block, piece, core)

    wsends = [0]

    def ring_send(block, sub, peer):
        ref = wt.at[block, sub]
        send(ref, ref, wsend.at[wsends[0]], wrecv.at[block, sub], peer)
        wsends[0] += 1

    def ring_start():
        for j in (1, 2, 3):
            block = lax.rem(x + j, NX)
            arrived(wx.at[block], wxsend.at[0], wxrecv.at[block])
        own_w = jnp.concatenate([wx[j] for j in range(NX)], axis=0).T
        for sub in range(2):
            wt[z, sub] = own_w[sub * 128:(sub + 1) * 128]
            ring_send(z, sub, zp)
            ring_send(z, sub, zm)

    def ring_step(k):
        for sub in range(2):
            block = lax.rem(z - k + NZ, NZ)
            arrived(wt.at[block, sub], wsend.at[0], wrecv.at[block, sub])
            if k < NZ // 2:
                ring_send(block, sub, zp)
            if k < NZ // 2:
                block = lax.rem(z + k, NZ)
                arrived(wt.at[block, sub], wsend.at[0], wrecv.at[block, sub])
                if k < NZ // 2 - 1:
                    ring_send(block, sub, zm)

    for copy in loads[3:]:
        copy.wait()
    ends, total = [], 0
    for j in range(8):
        total = total + dl_ref[0, j]
        ends.append(total)

    def segments(places):
        seg = jnp.zeros(places.shape, I32)
        for end in ends:
            seg = seg + (places >= end).astype(I32)
        return seg

    seg_s[...] = segments(spots)
    spot_s[...] = spots * jnp.int32(374761393)
    qt_s[...] = q_ref[...].T
    kt_s[...] = k_ref[...].T
    vt_s[...] = v_ref[...].T
    head_rows = lax.broadcasted_iota(I32, (FEAT, SEQ), 0) // DK
    head_lanes = lax.broadcasted_iota(I32, (SEQ, FEAT), 1) // DK
    ROWS = 64

    def forward(h):
        mine = jnp.where(head_rows == h, qt_s[...].astype(F32), 0.0).astype(BF)
        s_s[...] = jnp.dot(k_ref[...], mine, preferred_element_type=F32)

        def tile(t, carry):
            lanes = pl.ds(pl.multiple_of(t * 128, 128), 128)
            here = lax.broadcasted_iota(I32, (1, 128), 1) + t * 128
            seg_here = segments(here)
            word_here = here * jnp.int32(668265263) + ka_ref[0, h] * jnp.int32(-1640531535)
            top = jnp.full((ROWS, 128), -1e30, F32)
            for r in range(0, SEQ, ROWS):
                rows = pl.ds(r, ROWS)
                got = jnp.where(seg_s[rows, :] == seg_here, s_s[rows, lanes], -1e30)
                s_s[rows, lanes] = got
                top = jnp.maximum(top, got)
            top = jnp.max(top, axis=0, keepdims=True)
            mass = jnp.zeros((ROWS, 128), F32)
            for r in range(0, SEQ, ROWS):
                rows = pl.ds(r, ROWS)
                got = jnp.exp(s_s[rows, lanes] - top)
                s_s[rows, lanes] = got
                mass = mass + got
            scale = DROP_SCALE / jnp.sum(mass, axis=0, keepdims=True)
            for r in range(0, SEQ, ROWS):
                rows = pl.ds(r, ROWS)
                keep = kept_bits(spot_s[rows, :] + word_here)
                got = s_s[rows, lanes] * scale
                sp_s[h, rows, lanes] = jnp.where(keep, got, -got)
                kp_s[h, rows, lanes] = jnp.where(keep, got, 0.0).astype(BF)
            return carry

        lax.fori_loop(0, 4, tile, 0)
        ctxf[pl.ds(h * DK, DK), :] = jnp.dot(vt_s[pl.ds(h * DK, DK), :], kp_s[h], preferred_element_type=F32)

    def backward(h):
        mine = jnp.where(head_rows == h, gt_s[...].astype(F32), 0.0).astype(BF)
        s_s[...] = jnp.dot(v_ref[...], mine, preferred_element_type=F32)
        rows_h = pl.ds(h * DK, DK)
        delta = DROP * jnp.sum(gt_s[rows_h, :].astype(F32) * ctxf[rows_h, :], axis=0, keepdims=True)
        for t in range(4):
            lanes = pl.ds(t * 128, 128)
            for r in range(0, SEQ, ROWS):
                rows = pl.ds(r, ROWS)
                d = jnp.broadcast_to(delta[:, t * 128:(t + 1) * 128], (ROWS, 128))
                got = sp_s[h, rows, lanes]
                gs_s[rows, lanes] = (got * jnp.where(got > 0.0, s_s[rows, lanes] - d, d)).astype(BF)
        gqt_s[rows_h, :] = jnp.dot(kt_s[rows_h, :], gs_s[...], preferred_element_type=F32).astype(BF)
        q_h = jnp.where(head_lanes == h, q_ref[...].astype(F32), 0.0).astype(BF)
        g_h = jnp.where(head_lanes == h, g_s[...].astype(F32), 0.0).astype(BF)
        gk = jnp.dot(gs_s[...], q_h, preferred_element_type=F32)
        gv = jnp.dot(kp_s[h], g_h, preferred_element_type=F32)
        if h == 0:
            gka[...] = gk
            gva[...] = gv
        else:
            gka[...] += gk
            gva[...] += gv

    def dispatch(dy, u):
        to = lax.rem(y + dy + NY, NY)
        for piece in (2 * u, 2 * u + 1):
            ywait(yblock(dy, 1), piece)
        for half in range(2):
            for piece in (2 * u, 2 * u + 1):
                got = jnp.dot(drt[to * 2 + half, piece], ctx[...], preferred_element_type=F32)
                shr[to, half, pl.ds(piece * 128, 128), :] = got.astype(BF)
        dx = lax.rem(to - x + NX, NX)

        @pl.when(dx == 2)
        def _():
            for side in range(2):
                hop_copy(side, u).start()

        @pl.when(dx == 1)
        def _():
            early_copy(0, u).start()

        @pl.when(dx == 3)
        def _():
            early_copy(1, u).start()

    def x_copy(src, dst, slot, peer):
        return pltpu.make_async_remote_copy(
            src_ref=src, dst_ref=dst, send_sem=xsend.at[slot], recv_sem=xrecv.at[slot],
            device_id=peer, device_id_type=MESH,
        )

    def part_of(dx, half, u):
        return shr.at[lax.rem(x + dx + NX, NX), half, pl.ds(u * 256 if isinstance(u, int) else pl.multiple_of(u * 256, 256), 256)]

    def hop_copy(side, u):
        return x_copy(part_of(2, side, u), hop_r.at[side, u], 2 * side + u, (xp, xm)[side])

    def early_copy(side, u):
        if side == 0:
            return x_copy(part_of(1, 1, u), fin_r.at[0, u], 4 + u, xp)
        return x_copy(part_of(-1, 0, u), fin_r.at[1, u], 6 + u, xm)

    def late_copy(side, u):
        return x_copy(fin_s.at[side, u], fin_r.at[2 + side, u], 8 + 2 * side + u, (xp, xm)[side])

    def hop_step(side, u):
        hop_copy(side, u).wait_recv()
        mine = part_of((1, -1)[side], side, u)
        fin_s[side, u] = (mine[...].astype(F32) + hop_r[side, u].astype(F32)).astype(BF)
        late_copy(side, u).start()

    def near_copy(group, i):
        j = i + 1
        return pltpu.make_async_remote_copy(
            src_ref=near_s.at[group, lax.rem(near + j, NEAR)], dst_ref=near_r.at[group, near],
            send_sem=nsend.at[group, i], recv_sem=nrecv.at[group, near], device_id=near_peers[i], device_id_type=MESH,
        )

    def fin_step(half, u):
        group = 2 * half + u
        early_copy(1 - half, u).wait_recv()
        late_copy(half, u).wait_recv()
        total = part_of(0, half, u)[...].astype(F32)
        total = total + fin_r[1 - half, u].astype(F32) + fin_r[2 + half, u].astype(F32)
        near_s[group] = total.astype(BF).reshape(NEAR, DK, FEAT)
        for i in range(NEAR - 1):
            near_copy(group, i).start()

    def far_copy(group):
        return pltpu.make_async_remote_copy(
            src_ref=far_s.at[group], dst_ref=far_r.at[far], send_sem=fsend.at[group], recv_sem=frecv.at[far],
            device_id=(x * NZ + group * NEAR + near, mp), device_id_type=MESH,
        )

    def near_step(group):
        total = near_s[group, near].astype(F32)
        for j in range(1, NEAR):
            slot = lax.rem(near + j, NEAR)
            arrived(near_r.at[group, slot], nsend.at[0, 0], nrecv.at[group, slot])
            total = total + near_r[group, slot].astype(F32)
        far_s[group] = total.astype(BF)

        @pl.when(far != group)
        def _():
            far_copy(group).start()

    def context_part(block):
        half, piece, row = block // 8, (block % 8) // 2, (block % 2) * DK
        left = jnp.concatenate([wt[block, sub] for sub in range(2)], axis=0)
        right = jnp.concatenate([drt[2 * j + half, piece, pl.ds(row, DK), :] for j in range(NX)], axis=0)
        return jnp.dot(left, right, preferred_element_type=F32)

    forward(0)
    ring_start()
    forward(1)
    y_step(-1, 0)
    y_step(1, 2)
    ring_step(1)
    forward(2)
    y_step(-1, 1)
    y_step(1, 3)
    ysend_to(mp, 2, yp)
    ysend_to(mp, 0, ym)
    forward(3)
    ctx[...] = ctxf[...].astype(BF).T
    ring_step(2)
    dispatch(0, 0)
    dispatch(0, 1)
    dispatch(-1, 0)
    dispatch(1, 1)
    ysend_to(mp, 3, yp)
    ysend_to(mp, 1, ym)
    y_step(2, 0)
    y_step(2, 2)
    ring_step(3)
    y_step(2, 1)
    y_step(2, 3)
    dispatch(2, 0)
    dispatch(2, 1)
    y_step(-1, 2)
    y_step(1, 0)
    ring_step(4)
    y_step(-1, 3)
    y_step(1, 1)
    dispatch(-1, 1)
    dispatch(1, 0)
    ring_step(5)
    hop_first = (jnp.where(role == 2, 0, 1), jnp.where(role == 2, 1, 0))
    fin_first = (jnp.where(role == 1, 0, 1), jnp.where(role == 3, 1, 0))
    for side in range(2):
        hop_step(side, hop_first[side])
    for side in range(2):
        hop_step(side, 1 - hop_first[side])
    ring_step(6)
    for half in range(2):
        fin_step(half, fin_first[half])
    ring_step(7)
    for half in range(2):
        fin_step(half, 1 - fin_first[half])
    ring_step(8)
    acc = context_part(0)
    for block in range(1, NZ):
        acc = acc + context_part(block)
    gt_s[...] = acc.astype(BF)
    for half in range(2):
        near_step(2 * half + fin_first[half])
    for half in range(2):
        near_step(2 * half + 1 - fin_first[half])
    g_s[...] = gt_s[...].T
    for h in range(HEADS):
        backward(h)
    gq_ref[...] = gqt_s[...].T
    gk_ref[...] = gka[...].astype(BF)
    gv_ref[...] = gva[...].astype(BF)
    stores = [
        pltpu.make_async_copy(src, dst, store.at[i])
        for i, (src, dst) in enumerate(((gq_ref, gq_hbm), (gk_ref, gk_hbm), (gv_ref, gv_hbm), (gw_ref, gw_hbm)))
    ]
    for copy in stores[:3]:
        copy.start()
    total = far_s[far].astype(F32)
    for j in range(1, NEAR):
        slot = lax.rem(far + j, NEAR)
        arrived(far_r.at[slot], fsend.at[0], frecv.at[slot])
        total = total + far_r[slot].astype(F32)
    gw_ref[...] = total
    stores[3].start()
    for copy in pending:
        copy.wait_send()
    for copy in stores:
        copy.wait()
    for u in range(2):
        for side in range(2):
            hop_copy(side, u).wait_send()
            early_copy(side, u).wait_send()
            late_copy(side, u).wait_send()
    for group in range(NEAR):
        for i in range(NEAR - 1):
            near_copy(group, i).wait_send()

        @pl.when(far != group)
        def _(group=group):
            far_copy(group).wait_send()


def hand_over(*refs):
    load, store = refs[12:]
    loads = [pltpu.make_async_copy(refs[i], refs[8 + i], load.at[i]) for i in range(4)]
    stores = [pltpu.make_async_copy(refs[8 + i], refs[4 + i], store.at[i]) for i in range(4)]
    for copy in loads:
        copy.start()
    for i in range(4):
        loads[i].wait()
        stores[i].start()
    for copy in stores:
        copy.wait()


def shards(query, key, value, cotangent, weight_out, keep_attn, keep_out, doc_lengths):
    hbm = pl.BlockSpec(memory_space=pltpu.HBM)
    v, dma = pltpu.VMEM, pltpu.SemaphoreType.DMA
    grads = pl.pallas_call(
        kernel,
        name="attention_backward",
        out_shape=(
            jax.ShapeDtypeStruct((SEQ, FEAT), BF),
            jax.ShapeDtypeStruct((SEQ, FEAT), BF),
            jax.ShapeDtypeStruct((SEQ, FEAT), BF),
            jax.ShapeDtypeStruct((DK, FEAT), F32),
        ),
        in_specs=[hbm] * 8,
        out_specs=(hbm,) * 4,
        scratch_shapes=[
            v((SEQ, FEAT), BF),
            v((SEQ, FEAT), BF),
            v((SEQ, FEAT), BF),
            v((SEQ, SEQ), BF),
            v((DK, FEAT), BF),
            pltpu.SMEM((1, HEADS), I32),
            v((1, SEQ), I32),
            pltpu.SMEM((1, 8), I32),
            v((8, PIECES, 128, SEQ), BF),
            v((NX, DK, FEAT), BF),
            v((NZ, 2, 128, FEAT), BF),
            v((FEAT, SEQ), BF),
            v((FEAT, SEQ), BF),
            v((FEAT, SEQ), BF),
            v((FEAT, SEQ), BF),
            v((SEQ, FEAT), BF),
            v((FEAT, SEQ), F32),
            v((SEQ, FEAT), BF),
            v((SEQ, 128), I32),
            v((SEQ, 128), I32),
            v((SEQ, SEQ), F32),
            v((HEADS, SEQ, SEQ), F32),
            v((HEADS, SEQ, SEQ), BF),
            v((SEQ, SEQ), BF),
            v((FEAT, SEQ), BF),
            v((SEQ, FEAT), F32),
            v((SEQ, FEAT), F32),
            v((NX, 2, SEQ, FEAT), BF),
            v((2, 2, 256, FEAT), BF),
            v((2, 2, 256, FEAT), BF),
            v((4, 2, 256, FEAT), BF),
            v((4, NEAR, DK, FEAT), BF),
            v((4, NEAR, DK, FEAT), BF),
            v((4, DK, FEAT), BF),
            v((4, DK, FEAT), BF),
            v((SEQ, FEAT), BF),
            v((SEQ, FEAT), BF),
            v((SEQ, FEAT), BF),
            v((DK, FEAT), F32),
            dma((8,)), dma((4,)),
            dma((28,)), dma((8, PIECES)),
            dma((3,)), dma((NX,)),
            dma((32,)), dma((NZ, 2)),
            dma((12,)), dma((12,)),
            dma((4, 3)), dma((4, NEAR)),
            dma((4,)), dma((4,)),
        ],
        compiler_params=pltpu.CompilerParams(
            collective_id=0, has_side_effects=True, vmem_limit_bytes=60 * 2**20
        ),
    )(query, key, value, cotangent, weight_out, keep_attn.reshape(1, HEADS), keep_out, doc_lengths)
    return pl.pallas_call(
        hand_over,
        name="hand_over",
        out_shape=tuple(jax.ShapeDtypeStruct(g.shape, g.dtype) for g in grads),
        in_specs=[hbm] * 4,
        out_specs=(hbm,) * 4,
        scratch_shapes=[v(g.shape, g.dtype) for g in grads] + [dma((4,)), dma((4,))],
        compiler_params=pltpu.CompilerParams(vmem_limit_bytes=60 * 2**20),
    )(*grads)


def solution(mesh):
    in_specs = (
        P("dp", "mp"),
        P("dp", "mp"),
        P("dp", "mp"),
        P("dp", "mp"),
        P("dp", "mp"),
        P("mp", "dp"),
        P("dp", "mp"),
        P("dp", None),
    )
    out_specs = (P("dp", "mp"), P("dp", "mp"), P("dp", "mp"), P("dp", "mp"))
    return jax.shard_map(shards, mesh=mesh, in_specs=in_specs, out_specs=out_specs, check_vma=False)
```
